32 devices in a mesh: ma: 8 (over z, x), ao: 4 (over y, core).
Axes of the slice: x: 2, y: 2, z: 4, core: 2. Of those that a mesh axis runs over, the one named last changes fastest.
Arguments:
- truth_table: bfloat16 [4, 512, 512, 128], P('ao', 'ma'), may hold values from -1 to 1, as said below
- pair_list: int32 [4], replicated, may hold values from 0 to 3, as said below
Outputs:
- cross_corr: float32 [4, 512, 512, 128], P('ao', 'ma')
The draws below stay inside these ranges and needn't reach their ends.
Inputs may be any that keep to these rules, and one draw needn't show every extreme that they name: `truth_table`: every entry is +1 or -1. `pair_list`: each output's partner is another output, and every output is the partner of exactly one output.
All inputs are finite; a program needn't handle non-finite values.
Results may differ from the reference program's by a relative error of at most 0.0003.
Values sent between devices are 32-bit elements; how exact they have to be, the bound alone decides.
A program may use at most 192 MiB of HBM per device.

```python
import jax
import jax.numpy as jnp
from jax import lax

NA = 512
NB = 512
NC = 128
OUTS = 4


def draw_truth_table(key, part):
    values = jax.random.randint(key, (OUTS, NA, NB, NC), 0, 2)
    return (2 * values - 1).astype(jnp.float32).astype(jnp.bfloat16)


def draw_pair_list(key, part):
    order = jax.random.permutation(jax.random.fold_in(key, 7), OUTS).astype(jnp.int32)
    partner = jnp.zeros((OUTS,), jnp.int32).at[order].set(jnp.roll(order, -1))
    return partner


def setup_inputs(seed: int = 0) -> dict:
    key_of = jax.random.split(jax.random.key(seed), 3)
    truth_table = draw_truth_table(jax.random.fold_in(key_of[2], 71), 0)
    pair_list = draw_pair_list(jax.random.fold_in(key_of[2], 71), 0)
    return dict(truth_table=truth_table, pair_list=pair_list)


def sylvester(length):
    index_row = jnp.arange(length, dtype=jnp.int32)
    shared = jnp.bitwise_and(index_row[:, None], index_row[None, :])
    ones_count = jnp.zeros((length, length), jnp.int32)
    for position in range(length.bit_length() - 1):
        ones_count = ones_count + jnp.bitwise_and(jnp.right_shift(shared, position), 1)
    return (1 - 2 * (ones_count % 2)).astype(jnp.float32)

def walsh(field, h_high, h_mid, h_low):
    highest = lax.Precision.HIGHEST
    field = jnp.einsum('abj,jc->abc', field, h_low, precision=highest)
    field = jnp.einsum('bj,ajc->abc', h_mid, field, precision=highest)
    field = jnp.einsum('ai,ibc->abc', h_high, field, precision=highest)
    return field * (1.0 / jnp.sqrt(jnp.float32(NA * NB * NC)))

def reference(truth_table, pair_list):
    h_high = sylvester(NA)
    h_mid = sylvester(NB)
    h_low = sylvester(NC)
    spectra = lax.map(lambda table: walsh(table.astype(jnp.float32), h_high, h_mid, h_low), truth_table)

    def correlate(output):
        mate = pair_list[output]
        product = spectra[output] * spectra[mate]
        return walsh(product, h_high, h_mid, h_low)
    return lax.map(correlate, jnp.arange(OUTS, dtype=jnp.int32))
```

```python
import jax
import jax.numpy as jnp
from jax import lax
from jax.sharding import PartitionSpec as P

BOTH = ("ma", "ao")


def sylvester(length):
    index_row = jnp.arange(length, dtype=jnp.int32)
    shared = jnp.bitwise_and(index_row[:, None], index_row[None, :])
    ones_count = jnp.zeros((length, length), jnp.int32)
    for position in range(length.bit_length() - 1):
        ones_count = ones_count + jnp.bitwise_and(jnp.right_shift(shared, position), 1)
    return (1 - 2 * (ones_count % 2)).astype(jnp.bfloat16)


def halves(field):
    upper = lax.reduce_precision(field, 8, 7)
    lower = field - upper
    return upper.astype(jnp.bfloat16), lower.astype(jnp.bfloat16)


def product_of(spec, field, h):
    upper, lower = halves(field)
    one = jnp.einsum(spec, h, upper, preferred_element_type=jnp.float32)
    return one + jnp.einsum(spec, h, lower, preferred_element_type=jnp.float32)


def body(truth_table, pair_list):
    table = truth_table[0]
    rows, mid, low = table.shape
    n_ma, n_ao = lax.axis_size("ma"), lax.axis_size("ao")
    devices = n_ma * n_ao
    high = rows * n_ma
    share = mid // devices
    factor = 1.0 / jnp.sqrt(jnp.float32(high * mid * low))
    h_high, h_mid, h_low = sylvester(high), sylvester(mid), sylvester(low)

    first = jnp.einsum("abj,jc->abc", table, h_low, preferred_element_type=jnp.float32)
    first = first.astype(jnp.bfloat16)
    h_parts = h_mid.reshape(devices, share, mid)
    partial = jnp.einsum("dbj,ajc->dabc", h_parts, first, preferred_element_type=jnp.float32)
    here = lax.all_to_all(partial, BOTH, split_axis=0, concat_axis=0, tiled=True)
    here = here.reshape(n_ma, n_ao, rows, share, low)
    here = here.transpose(1, 0, 2, 3, 4).reshape(n_ao, high, share * low)
    spectrum = product_of("hi,oir->ohr", here, h_high) * factor
    mates = jnp.stack(
        [
            lax.dynamic_index_in_dim(spectrum, pair_list[o], 0, keepdims=False)
            for o in range(n_ao)
        ]
    )
    product = spectrum * mates
    mixed = product_of("hi,oir->ohr", product, h_high) * factor
    mixed = mixed.reshape(n_ao, n_ma, rows * share, low)
    mixed = product_of("cj,omrj->omrc", mixed, h_low)
    mixed = mixed.reshape(n_ao, n_ma, rows, share, low).transpose(1, 0, 2, 3, 4)
    mixed = mixed.reshape(devices, rows, share, low)
    back = lax.all_to_all(mixed, BOTH, split_axis=0, concat_axis=0, tiled=True)
    h_parts = h_mid.reshape(mid, devices, share)
    return product_of("bdj,dajc->abc", back, h_parts)[None]


def solution(mesh):
    return jax.shard_map(
        body,
        mesh=mesh,
        in_specs=(P("ao", "ma", None, None), P()),
        out_specs=P("ao", "ma", None, None),
        check_vma=False,
    )
```

```python
import functools

import jax
import jax.numpy as jnp
from jax import lax
from jax.experimental import pallas as pl
from jax.experimental.pallas import tpu as pltpu
from jax.sharding import PartitionSpec as P

BOTH = ("ma", "ao")
VMEM_LIMIT = 56 * 1024 * 1024
CHUNKS = 1


def sylvester(length):
    index_row = jnp.arange(length, dtype=jnp.int32)
    shared = jnp.bitwise_and(index_row[:, None], index_row[None, :])
    ones_count = jnp.zeros((length, length), jnp.int32)
    for position in range(length.bit_length() - 1):
        ones_count = ones_count + jnp.bitwise_and(jnp.right_shift(shared, position), 1)
    return (1 - 2 * (ones_count % 2)).astype(jnp.bfloat16)


def halves(field):
    upper = field.astype(jnp.bfloat16)
    lower = (field - upper.astype(jnp.float32)).astype(jnp.bfloat16)
    return upper, lower


def dot(a, b):
    return jnp.dot(a, b, preferred_element_type=jnp.float32)


def left_product(h, field):
    upper, lower = halves(field)
    return dot(h, upper) + dot(h, lower)


def first_kernel(table_ref, mid_ref, low_ref, *out_refs):
    rows, mid, low = table_ref.shape
    devices, _, share, _ = out_refs[0].shape
    h_mid, h_low = mid_ref[...], low_ref[...]
    for a in range(0, rows, 2):
        pair = [dot(table_ref[a + k], h_low).astype(jnp.bfloat16) for k in range(2)]
        both = dot(h_mid, jnp.concatenate(pair, axis=1))
        for k in range(2):
            one = both[:, k * low:(k + 1) * low]
            one = one.reshape(devices, len(out_refs) * share, low)
            for c, out_ref in enumerate(out_refs):
                out_ref[:, a + k] = one[:, c * share:(c + 1) * share]


def middle_kernel(factor, pair_ref, in_ref, high_ref, low_ref, out_ref, spec_ref):
    n_ma, n_ao, rows, share, low = in_ref.shape
    high = n_ma * rows
    h_high = high_ref[...]
    h_low2 = jnp.concatenate([low_ref[...]] * 2, axis=0)
    for m in range(share):
        field = jnp.concatenate(
            [in_ref[:, o, :, m, :].reshape(high, low) for o in range(n_ao)], axis=1
        )
        spectrum = left_product(h_high, field) * factor
        for o in range(n_ao):
            spec_ref[o] = spectrum[:, o * low:(o + 1) * low]
        product = jnp.concatenate(
            [
                spec_ref[o] * spec_ref[jnp.clip(pair_ref[o], 0, n_ao - 1)]
                for o in range(n_ao)
            ],
            axis=1,
        )
        mixed = left_product(h_high, product) * factor
        for o in range(n_ao):
            parts = halves(mixed[:, o * low:(o + 1) * low])
            done = dot(jnp.concatenate(parts, axis=1), h_low2)
            out_ref[:, o, :, m, :] = done.reshape(n_ma, rows, low)


def last_kernel(mid_ref, *refs):
    *in_refs, out_ref = refs
    rows, mid, low = out_ref.shape
    h_mid = mid_ref[...]
    for a in range(0, rows, 2):
        pair = []
        for k in range(2):
            parts = [ref[:, a + k] for ref in in_refs]
            one = parts[0] if len(parts) == 1 else jnp.concatenate(parts, axis=1)
            pair.append(one.reshape(mid, low))
        both = left_product(h_mid, jnp.concatenate(pair, axis=1))
        for k in range(2):
            out_ref[a + k] = both[:, k * low:(k + 1) * low]


def params():
    return pltpu.CompilerParams(vmem_limit_bytes=VMEM_LIMIT)


def whole(array):
    return pl.BlockSpec(array.shape, lambda i: (0,) * array.ndim)


def body(truth_table, pair_list):
    table = truth_table[0]
    rows, mid, low = table.shape
    n_ma, n_ao = lax.axis_size("ma"), lax.axis_size("ao")
    devices = n_ma * n_ao
    high = rows * n_ma
    share = mid // devices
    chunks = CHUNKS if share % (8 * CHUNKS) == 0 else 1
    part = share // chunks
    step = min(8, rows)
    block = min(8, part)
    factor = float(1.0 / (high * mid * low) ** 0.5)
    h_high, h_mid, h_low = sylvester(high), sylvester(mid), sylvester(low)
    sent = jax.ShapeDtypeStruct((devices, rows, part, low), jnp.float32)
    rows_spec = pl.BlockSpec((devices, step, part, low), lambda i: (0, i, 0, 0))
    table_spec = pl.BlockSpec((step, mid, low), lambda i: (i, 0, 0))

    partial = pl.pallas_call(
        first_kernel,
        grid=(rows // step,),
        in_specs=[table_spec, whole(h_mid), whole(h_low)],
        out_specs=[rows_spec] * chunks,
        out_shape=[sent] * chunks,
        compiler_params=params(),
        cost_estimate=pl.CostEstimate(
            flops=2 * rows * mid * low * (mid + low),
            bytes_accessed=6 * rows * mid * low,
            transcendentals=0,
        ),
    )(table, h_mid, h_low)

    five = (n_ma, n_ao, rows, part, low)
    five_spec = pl.BlockSpec((n_ma, n_ao, rows, block, low), lambda i: (0, 0, 0, i, 0))
    middle = pl.pallas_call(
        functools.partial(middle_kernel, factor),
        grid=(part // block,),
        in_specs=[
            pl.BlockSpec(memory_space=pltpu.SMEM),
            five_spec,
            whole(h_high),
            whole(h_low),
        ],
        out_specs=five_spec,
        out_shape=jax.ShapeDtypeStruct(five, jnp.float32),
        scratch_shapes=[pltpu.VMEM((n_ao, high, low), jnp.float32)],
        compiler_params=params(),
        cost_estimate=pl.CostEstimate(
            flops=8 * n_ao * high * part * low * high,
            bytes_accessed=8 * n_ao * high * part * low,
            transcendentals=0,
        ),
    )

    back = []
    for piece in partial:
        here = lax.all_to_all(piece, BOTH, split_axis=0, concat_axis=0, tiled=True)
        mixed = middle(pair_list, here.reshape(five), h_high, h_low)
        mixed = mixed.reshape(devices, rows, part, low)
        back.append(lax.all_to_all(mixed, BOTH, split_axis=0, concat_axis=0, tiled=True))

    result = pl.pallas_call(
        last_kernel,
        grid=(rows // step,),
        in_specs=[whole(h_mid)] + [rows_spec] * chunks,
        out_specs=table_spec,
        out_shape=jax.ShapeDtypeStruct((rows, mid, low), jnp.float32),
        compiler_params=params(),
        cost_estimate=pl.CostEstimate(
            flops=4 * rows * mid * low * mid,
            bytes_accessed=8 * rows * mid * low,
            transcendentals=0,
        ),
    )(h_mid, *back)
    return result[None]


def solution(mesh):
    return jax.shard_map(
        body,
        mesh=mesh,
        in_specs=(P("ao", "ma", None, None), P()),
        out_specs=P("ao", "ma", None, None),
        check_vma=False,
    )
```

```python
import functools

import jax
import jax.numpy as jnp
from jax import lax
from jax.experimental import pallas as pl
from jax.experimental.pallas import tpu as pltpu
from jax.sharding import PartitionSpec as P

BOTH = ("ma", "ao")
VMEM_LIMIT = 56 * 1024 * 1024
CHUNKS = 2


def sylvester(length):
    index_row = jnp.arange(length, dtype=jnp.int32)
    shared = jnp.bitwise_and(index_row[:, None], index_row[None, :])
    ones_count = jnp.zeros((length, length), jnp.int32)
    for position in range(length.bit_length() - 1):
        ones_count = ones_count + jnp.bitwise_and(jnp.right_shift(shared, position), 1)
    return (1 - 2 * (ones_count % 2)).astype(jnp.bfloat16)


def halves(field):
    upper = field.astype(jnp.bfloat16)
    lower = (field - upper.astype(jnp.float32)).astype(jnp.bfloat16)
    return upper, lower


def dot(a, b):
    return jnp.dot(a, b, preferred_element_type=jnp.float32)


def left_product(h, field):
    upper, lower = halves(field)
    return dot(h, upper) + dot(h, lower)


def first_kernel(table_ref, mid_ref, low_ref, *out_refs):
    rows, mid, low = table_ref.shape
    devices, _, share, _ = out_refs[0].shape
    h_mid, h_low = mid_ref[...], low_ref[...]
    for a in range(0, rows, 2):
        pair = [dot(table_ref[a + k], h_low).astype(jnp.bfloat16) for k in range(2)]
        both = dot(h_mid, jnp.concatenate(pair, axis=1))
        for k in range(2):
            one = both[:, k * low:(k + 1) * low]
            one = one.reshape(devices, len(out_refs) * share, low)
            for c, out_ref in enumerate(out_refs):
                out_ref[:, a + k] = one[:, c * share:(c + 1) * share]


def middle_kernel(factor, pair_ref, in_ref, high_ref, low_ref, out_ref, spec_ref):
    n_ma, n_ao, rows, share, low = in_ref.shape
    high = n_ma * rows
    h_high = high_ref[...]
    h_low2 = jnp.concatenate([low_ref[...]] * 2, axis=0)
    for m in range(share):
        field = jnp.concatenate(
            [in_ref[:, o, :, m, :].reshape(high, low) for o in range(n_ao)], axis=1
        )
        spectrum = left_product(h_high, field) * factor
        for o in range(n_ao):
            spec_ref[o] = spectrum[:, o * low:(o + 1) * low]
        product = jnp.concatenate(
            [
                spec_ref[o] * spec_ref[jnp.clip(pair_ref[o], 0, n_ao - 1)]
                for o in range(n_ao)
            ],
            axis=1,
        )
        mixed = left_product(h_high, product) * factor
        for o in range(n_ao):
            parts = halves(mixed[:, o * low:(o + 1) * low])
            done = dot(jnp.concatenate(parts, axis=1), h_low2)
            out_ref[:, o, :, m, :] = done.reshape(n_ma, rows, low)


def last_kernel(mid_ref, *refs):
    *in_refs, out_ref = refs
    rows, mid, low = out_ref.shape
    h_mid = mid_ref[...]
    for a in range(0, rows, 2):
        pair = []
        for k in range(2):
            parts = [ref[:, a + k] for ref in in_refs]
            one = parts[0] if len(parts) == 1 else jnp.concatenate(parts, axis=1)
            pair.append(one.reshape(mid, low))
        both = left_product(h_mid, jnp.concatenate(pair, axis=1))
        for k in range(2):
            out_ref[a + k] = both[:, k * low:(k + 1) * low]


def params():
    return pltpu.CompilerParams(vmem_limit_bytes=VMEM_LIMIT)


def whole(array):
    return pl.BlockSpec(array.shape, lambda i: (0,) * array.ndim)


def body(truth_table, pair_list):
    table = truth_table[0]
    rows, mid, low = table.shape
    n_ma, n_ao = lax.axis_size("ma"), lax.axis_size("ao")
    devices = n_ma * n_ao
    high = rows * n_ma
    share = mid // devices
    chunks = CHUNKS if share % (8 * CHUNKS) == 0 else 1
    part = share // chunks
    step = min(8, rows)
    block = min(8, part)
    factor = float(1.0 / (high * mid * low) ** 0.5)
    h_high, h_mid, h_low = sylvester(high), sylvester(mid), sylvester(low)
    sent = jax.ShapeDtypeStruct((devices, rows, part, low), jnp.float32)
    rows_spec = pl.BlockSpec((devices, step, part, low), lambda i: (0, i, 0, 0))
    table_spec = pl.BlockSpec((step, mid, low), lambda i: (i, 0, 0))

    partial = pl.pallas_call(
        first_kernel,
        grid=(rows // step,),
        in_specs=[table_spec, whole(h_mid), whole(h_low)],
        out_specs=[rows_spec] * chunks,
        out_shape=[sent] * chunks,
        compiler_params=params(),
        cost_estimate=pl.CostEstimate(
            flops=2 * rows * mid * low * (mid + low),
            bytes_accessed=6 * rows * mid * low,
            transcendentals=0,
        ),
    )(table, h_mid, h_low)

    five = (n_ma, n_ao, rows, part, low)
    five_spec = pl.BlockSpec((n_ma, n_ao, rows, block, low), lambda i: (0, 0, 0, i, 0))
    middle = pl.pallas_call(
        functools.partial(middle_kernel, factor),
        grid=(part // block,),
        in_specs=[
            pl.BlockSpec(memory_space=pltpu.SMEM),
            five_spec,
            whole(h_high),
            whole(h_low),
        ],
        out_specs=five_spec,
        out_shape=jax.ShapeDtypeStruct(five, jnp.float32),
        scratch_shapes=[pltpu.VMEM((n_ao, high, low), jnp.float32)],
        compiler_params=params(),
        cost_estimate=pl.CostEstimate(
            flops=8 * n_ao * high * part * low * high,
            bytes_accessed=8 * n_ao * high * part * low,
            transcendentals=0,
        ),
    )

    back = []
    for piece in partial:
        here = lax.all_to_all(piece, BOTH, split_axis=0, concat_axis=0, tiled=True)
        mixed = middle(pair_list, here.reshape(five), h_high, h_low)
        mixed = mixed.reshape(devices, rows, part, low)
        back.append(lax.all_to_all(mixed, BOTH, split_axis=0, concat_axis=0, tiled=True))

    result = pl.pallas_call(
        last_kernel,
        grid=(rows // step,),
        in_specs=[whole(h_mid)] + [rows_spec] * chunks,
        out_specs=table_spec,
        out_shape=jax.ShapeDtypeStruct((rows, mid, low), jnp.float32),
        compiler_params=params(),
        cost_estimate=pl.CostEstimate(
            flops=4 * rows * mid * low * mid,
            bytes_accessed=8 * rows * mid * low,
            transcendentals=0,
        ),
    )(h_mid, *back)
    return result[None]


def solution(mesh):
    return jax.shard_map(
        body,
        mesh=mesh,
        in_specs=(P("ao", "ma", None, None), P()),
        out_specs=P("ao", "ma", None, None),
        check_vma=False,
    )
```
